128 devices in a mesh: ctx: 32 (over y_hi, x, z), head: 4 (over y_lo, core).
Axes of the slice: x: 4, y: 4 (y_hi: 2, y_lo: 2; y = y_hi * 2 + y_lo), z: 4, core: 2. Of those that a mesh axis runs over, the one named last changes fastest.
Arguments:
- queries: bfloat16 [32, 256, 8192], P('ctx', None, 'head'), may hold values from -64 to 64
- keys: bfloat16 [131072, 8, 128], P('ctx', 'head'), may hold values from -6 to 6
- values: bfloat16 [131072, 8, 128], P('ctx', 'head'), may hold values from -6 to 6
- lengths: int32 [32], P('ctx'), may hold values from 1024 to 4096, as said below
- owner: int32 [1], replicated, may hold values from 0 to 31
- w_out: bfloat16 [8192, 8192], P('head', 'ctx'), may hold values from -0.0625 to 0.0625
Outputs:
- attended: bfloat16 [256, 8192], P(None, 'head')
- projected: bfloat16 [256, 8192], P('head', 'ctx')
The draws below stay inside these ranges and needn't reach their ends.
Inputs may be any that keep to these rules, and one draw needn't show every extreme that they name: `lengths`: some host's block is full.
All inputs are finite; a program needn't handle non-finite values.
Results may differ from the reference program's by a relative error of at most 0.015.
Values may be sent and summed in bfloat16 or wider, within the bound.
A program may use at most 256 MiB of HBM per device.

```python
import math
import jax
import jax.numpy as jnp
from jax import lax

HQ = 64
KVH = 8
HD = 128
D = 8192
QROWS = 256
CTX_DEV = 4096
KB = 512
HOSTS = 32
CONTEXT = 131072


def draw_keys(key, part):
    key = jax.random.fold_in(key, 7)
    cached = jnp.clip(jax.random.normal(key, (CONTEXT, KVH, HD), jnp.float32), -6.0, 6.0)
    return cached.astype(jnp.bfloat16)


def draw_queries(key, part):
    key = jax.random.fold_in(key, 9)
    rows_all = jnp.clip(2.0 * jax.random.normal(key, (HOSTS, QROWS, HQ, HD), jnp.float32), -12.0, 12.0)
    return rows_all.reshape(HOSTS, QROWS, HQ * HD).astype(jnp.bfloat16)


def draw_lengths(key, part):
    key = jax.random.fold_in(key, 5)
    first_key, second_key = jax.random.split(key)
    counts = jax.random.randint(first_key, (HOSTS,), CTX_DEV // 4, CTX_DEV + 1, jnp.int32)
    filled = jax.random.randint(second_key, (), 0, HOSTS, jnp.int32)
    counts = jnp.where(jnp.arange(HOSTS, dtype=jnp.int32) == filled, CTX_DEV, counts)
    return counts.astype(jnp.int32)


def levels(key, dims, cuts, least, high):
    loudness = 1.0
    for axis_at, blocks in cuts:
        heights = jax.random.uniform(jax.random.fold_in(jax.random.fold_in(key, 6), axis_at), (blocks,), jnp.float32, least / len(cuts), high / len(cuts))
        loudness = loudness * jnp.repeat(jnp.exp(heights), dims[axis_at] // blocks).reshape((-1,) + (1,) * (len(dims) - 1 - axis_at))
    return loudness


def scatter_about(key, extent, scale, most, pieces=(), kind=jnp.bfloat16):
    values = jax.random.normal(key, extent, jnp.float32) * scale
    if len(pieces) > 0:
        values = levels(key, extent, pieces, -0.22, 0.18) * values
    return jnp.clip(values, min=-most, max=most).astype(kind)


def setup_inputs(seed: int = 0) -> dict:
    key_list = jax.random.split(jax.random.key(seed), 7)
    queries = draw_queries(jax.random.fold_in(key_list[6], 71), 0)
    keys = draw_keys(jax.random.fold_in(key_list[6], 71), 0)
    values = scatter_about(key_list[2], (CONTEXT, KVH, HD), 1.0, 6.0, ((0, 32), (1, 4)))
    lengths = draw_lengths(jax.random.fold_in(key_list[6], 71), 0)
    owner = jax.random.randint(key_list[4], (1,), 0, HOSTS).astype(jnp.int32)
    w_out = scatter_about(key_list[5], (HQ * HD, D), (HQ * HD) ** -0.5, 0.0625, ((0, 4), (1, 32)))
    return dict(queries=queries, keys=keys, values=values, lengths=lengths, owner=owner, w_out=w_out)


NEGATIVE = -1e+30

def combine_partials(first_part, second_part):
    peak_first, total_first, weighted_first = first_part
    peak_second, total_second, weighted_second = second_part
    peak = jnp.maximum(peak_first, peak_second)
    factor_first = jnp.exp(peak_first - peak)
    factor_second = jnp.exp(peak_second - peak)
    total = total_first * factor_first + total_second * factor_second
    weighted = weighted_first * factor_first[..., None] + weighted_second * factor_second[..., None]
    return (peak, total, weighted)

def softmax_block(scores, usable):
    masked = jnp.where(usable, scores, NEGATIVE)
    peak = lax.optimization_barrier(jnp.max(masked, axis=-1))
    weights = jnp.where(usable, jnp.exp(scores - peak[..., None]), 0.0).astype(jnp.bfloat16)
    total = lax.optimization_barrier(jnp.sum(weights.astype(jnp.float32), axis=-1))
    return (peak, total, weights)

def reference(queries, keys, values, lengths, owner, w_out):
    chosen = lax.dynamic_index_in_dim(queries, owner[0], 0, keepdims=False)
    per_group = HQ // KVH
    grouped = chosen.reshape(QROWS, KVH, per_group, HD).astype(jnp.float32)
    per_host = CTX_DEV // KB
    key_sets = keys.reshape(HOSTS, per_host, KB, KVH, HD)
    value_sets = values.reshape(HOSTS, per_host, KB, KVH, HD)
    offsets = jnp.arange(per_host, dtype=jnp.int32) * KB
    score_scale = 1.0 / math.sqrt(HD)

    def host_step(carry, element):
        key_set, value_set, valid = element

        def absorb(running, inner):
            key_block, value_block, offset = inner
            usable = (offset + jnp.arange(KB, dtype=jnp.int32)).astype(jnp.int32) < valid
            scores = jnp.einsum('rgjd,kgd->gjrk', grouped, key_block.astype(jnp.float32)) * score_scale
            peak, total, weights = softmax_block(scores, usable)
            weighted = jnp.einsum('gjrk,kgd->gjrd', weights.astype(jnp.float32), value_block.astype(jnp.float32))
            return (combine_partials(running, (peak, total, weighted)), None)
        start = (jnp.full((KVH, per_group, QROWS), NEGATIVE, jnp.float32), jnp.zeros((KVH, per_group, QROWS), jnp.float32), jnp.zeros((KVH, per_group, QROWS, HD), jnp.float32))
        (peak, total, weighted), _ = lax.scan(absorb, start, (key_set, value_set, offsets))
        local = (weighted / total[..., None]).astype(jnp.bfloat16)
        lse = peak + jnp.log(total)
        top, denom, numer = carry
        new_top = jnp.maximum(top, lse)
        keep = jnp.exp(top - new_top)
        scale = jnp.exp(lse - new_top)
        denom = denom * keep + scale
        numer = numer * keep[..., None] + local.astype(jnp.float32) * scale[..., None]
        return ((new_top, denom, numer), None)
    begin = (jnp.full((KVH, per_group, QROWS), NEGATIVE, jnp.float32), jnp.zeros((KVH, per_group, QROWS), jnp.float32), jnp.zeros((KVH, per_group, QROWS, HD), jnp.float32))
    (top, denom, numer), _ = lax.scan(host_step, begin, (key_sets, value_sets, lengths))
    normed = (numer / denom[..., None]).astype(jnp.bfloat16)
    attended = normed.transpose(2, 0, 1, 3).reshape(QROWS, HQ * HD)
    projected = jnp.dot(attended, w_out, preferred_element_type=jnp.float32).astype(jnp.bfloat16)
    return (attended, projected)
```

```python
import functools
import math

import jax
import jax.numpy as jnp
from jax import lax
from jax.experimental import pallas as pl
from jax.experimental.pallas import tpu as pltpu
from jax.sharding import PartitionSpec as P

MESH = pl.DeviceIdType.MESH
HOSTS = 32
GROUPS = 8
ROWS = 256
HD = 128
KEYS = 4096
CHUNK = 1024
SCALE = math.log2(math.e) / math.sqrt(HD)
QB = 4
LAG = 2


def remote(src, dst, send, recv, ctx):
    return pltpu.make_async_remote_copy(
        src_ref=src, dst_ref=dst, send_sem=send, recv_sem=recv, device_id=ctx, device_id_type=MESH
    )


def drain(ref, sem):
    pltpu.make_async_copy(ref, ref, sem).wait()


def scatter_kernel(owner, q_ref, out_ref, send, recv):
    me = lax.axis_index("ctx")
    barrier = pltpu.get_barrier_semaphore()

    @pl.when(me != owner)
    def _():
        pl.semaphore_signal(barrier, inc=1, device_id={"ctx": owner}, device_id_type=MESH)
        drain(out_ref, recv)

    @pl.when(me == owner)
    def _():
        pl.semaphore_wait(barrier, HOSTS - 1)

        def piece(p):
            return q_ref.at[0, pl.ds(16 * (p % 16), 16), pl.ds(1024 * (p // 16), 1024)]

        copies = []
        for step in range(1, HOSTS):
            p = (owner + step) % HOSTS
            copies.append(remote(piece(p), out_ref, send.at[step], recv, {"ctx": p}))
            copies[-1].start()
        own = pltpu.make_async_copy(piece(owner), out_ref, send.at[0])
        own.start()
        own.wait()
        for copy in copies:
            copy.wait_send()


def scatter(owner, queries):
    return pl.pallas_call(
        functools.partial(scatter_kernel, owner),
        out_shape=jax.ShapeDtypeStruct((16, 1024), jnp.bfloat16),
        in_specs=[pl.BlockSpec(memory_space=pl.ANY)],
        out_specs=pl.BlockSpec(memory_space=pltpu.VMEM),
        scratch_shapes=[pltpu.SemaphoreType.DMA((HOSTS,)), pltpu.SemaphoreType.DMA],
        compiler_params=pltpu.CompilerParams(collective_id=owner + 1, has_side_effects=True),
    )(queries)


def main_kernel(
    qp_ref, k_hbm, v_hbm, len_ref, w_hbm, att_hbm, proj_ref,
    k_in, v_in, w_ref, k_ref, vt_ref, q_ref, sa, sb, o_buf, o_recv, l_buf, l_recv, at_piece, at_buf,
    part, hd_buf, hd_recv, local_sem, q_send, q_recv, o_send, o_rsem, l_send, l_rsem, a_send, a_recv, h_send, h_rsem,
):
    me = lax.axis_index("ctx")
    hd = lax.axis_index("head")
    my_kv, my_row = me // 16, lax.rem(me, 16)
    loads = [
        pltpu.make_async_copy(k_hbm, k_in, local_sem.at[0]),
        pltpu.make_async_copy(v_hbm, v_in, local_sem.at[1]),
        pltpu.make_async_copy(w_hbm, w_ref, local_sem.at[2]),
    ]
    for load in loads:
        load.start()
    barrier = pltpu.get_barrier_semaphore()

    def greet(i, _):
        pl.semaphore_signal(barrier, inc=1, device_id={"ctx": lax.rem(me + i, HOSTS)}, device_id_type=MESH)
        return _

    lax.fori_loop(1, HOSTS, greet, 0)
    for i in (1, 2, 3):
        pl.semaphore_signal(barrier, inc=1, device_id={"head": lax.rem(hd + i, 4)}, device_id_type=MESH)
    pl.semaphore_wait(barrier, HOSTS - 1 + 3)

    width = 1024 // QB
    for b in range(QB):
        cols = pl.ds(b * width, width)
        src = qp_ref.at[:, cols]
        dst = q_ref.at[my_kv, pl.ds(pl.multiple_of(16 * my_row, 16), 16), cols]

        def send_q(i, _):
            remote(src, dst, q_send.at[b], q_recv.at[b], {"ctx": lax.rem(me + i, HOSTS)}).start()
            return _

        lax.fori_loop(1, HOSTS, send_q, 0)
        pltpu.make_async_copy(src, dst, q_recv.at[b]).start()

    count = len_ref[0]
    loads[0].wait()
    for g in range(2):
        first = k_in[0:1, g, :]

        def prep_k(c, _):
            at = pl.multiple_of(c * 512, 512)
            row = lax.broadcasted_iota(jnp.int32, (512, HD), 0) + at
            k_ref[g, pl.ds(at, 512), :] = jnp.where(row < count, k_in[pl.ds(at, 512), g, :], first)
            return _

        lax.fori_loop(0, KEYS // 512, prep_k, 0)
    loads[1].wait()
    for g in range(2):

        def prep_v(c, _):
            at = pl.multiple_of(c * 512, 512)
            row = lax.broadcasted_iota(jnp.int32, (512, HD), 0) + at
            v = jnp.where(row < count, v_in[pl.ds(at, 512), g, :].astype(jnp.float32), 0.0)
            vt_ref[g, 0:HD, pl.ds(at, 512)] = v.T.astype(jnp.bfloat16)
            col = lax.broadcasted_iota(jnp.int32, (16, 512), 1) + at
            vt_ref[g, HD : HD + 16, pl.ds(at, 512)] = jnp.where(col < count, 1.0, 0.0).astype(jnp.bfloat16)
            return _

        lax.fori_loop(0, KEYS // 512, prep_v, 0)

    def head_q(g, kv):
        return q_ref[kv, :, pl.ds(pl.multiple_of(g * HD, HD), HD)]

    def scores(kv, c, q, s_ref, top):
        at = c * CHUNK
        s = lax.dot_general(
            k_ref[kv, at : at + CHUNK, :], q, (((1,), (1,)), ((), ())), preferred_element_type=jnp.float32
        )
        s_ref[at : at + CHUNK, :] = s
        return jnp.maximum(top, jnp.max(s.reshape(CHUNK // 8, 8, ROWS), axis=0))

    def weigh(kv, c, s_ref, top, acc):
        at = c * CHUNK
        p = jnp.exp2(s_ref[at : at + CHUNK, :] * SCALE - top).astype(jnp.bfloat16)
        return acc + jnp.dot(vt_ref[kv, 0 : HD + 8, at : at + CHUNK], p, preferred_element_type=jnp.float32)

    def finish(g, kv, acc, top):
        total = acc[HD : HD + 1]
        o_buf[g, kv] = (acc[:HD] / total).T.astype(jnp.bfloat16)
        lse = top + jnp.log2(total)
        l_buf[g, kv, 0] = lse[:, :128]
        l_buf[g, kv, 1] = lse[:, 128:]

    low = jnp.full((8, ROWS), -jnp.inf, jnp.float32)
    zero = jnp.zeros((HD + 8, ROWS), jnp.float32)

    def attend(g, best):
        top = jnp.max(best, axis=0, keepdims=True) * SCALE
        q = head_q(g, 1)
        other, acc = low, zero
        for c in range(KEYS // CHUNK):
            other = scores(1, c, q, sb, other)
            acc = weigh(0, c, sa, top, acc)
        finish(g, 0, acc, top)
        top = jnp.max(other, axis=0, keepdims=True) * SCALE
        q = head_q(jnp.minimum(g + 1, GROUPS - 1), 0)
        best, acc = low, zero
        for c in range(KEYS // CHUNK):
            best = scores(0, c, q, sa, best)
            acc = weigh(1, c, sb, top, acc)
        finish(g, 1, acc, top)
        return best

    def send_out(g):
        def one(i, _):
            p = lax.rem(me + i, HOSTS)
            kv, row = p // 16, lax.rem(p, 16)
            remote(
                o_buf.at[g, kv, pl.ds(pl.multiple_of(16 * row, 16), 16), :], o_recv.at[g, me],
                o_send.at[g], o_rsem.at[g], {"ctx": p},
            ).start()
            remote(l_buf.at[g, kv, row // 8], l_recv.at[g, me], l_send.at[g], l_rsem.at[g], {"ctx": p}).start()
            return _

        lax.fori_loop(1, HOSTS, one, 0)
        pltpu.make_async_copy(
            o_buf.at[g, my_kv, pl.ds(pl.multiple_of(16 * my_row, 16), 16), :], o_recv.at[g, me], o_rsem.at[g]
        ).start()
        pltpu.make_async_copy(l_buf.at[g, my_kv, my_row // 8], l_recv.at[g, me], l_rsem.at[g]).start()

    def combine(g):
        drain(l_recv.at[g], l_rsem.at[g])
        drain(o_recv.at[g], o_rsem.at[g])
        lse = l_recv[g, :, 0, :]
        w = jnp.exp2(lse - jnp.max(lse, axis=0, keepdims=True))
        w = w / jnp.sum(w, axis=0, keepdims=True)
        w = pltpu.roll(w, lax.rem(128 - 16 * lax.rem(my_row, 8), 128), 1)
        w = jnp.concatenate([w, jnp.zeros((96, 128), jnp.float32)], 0).T[:16]
        acc = jnp.zeros((16, HD), jnp.float32)
        for h in range(HOSTS):
            acc = acc + w[:, h : h + 1] * o_recv[g, h].astype(jnp.float32)
        at_piece[g] = acc.astype(jnp.bfloat16)
        cols = pl.ds(pl.multiple_of(g * HD, HD), HD)
        dst = at_buf.at[my_kv, pl.ds(pl.multiple_of(16 * my_row, 16), 16), cols]

        def one(i, _):
            remote(at_piece.at[g], dst, a_send.at[g], a_recv.at[g], {"ctx": lax.rem(me + i, HOSTS)}).start()
            return _

        lax.fori_loop(1, HOSTS, one, 0)
        pltpu.make_async_copy(at_piece.at[g], dst, a_recv.at[g]).start()

    def project(g):
        cols = pl.ds(pl.multiple_of(g * HD, HD), HD)
        drain(at_buf.at[:, :, cols], a_recv.at[g])
        for kv in range(2):
            rows = pl.ds(pl.multiple_of(kv * 1024 + g * HD, HD), HD)
            part[...] += jnp.dot(at_buf[kv, :, cols], w_ref[rows, :], preferred_element_type=jnp.float32)

    part[...] = jnp.zeros_like(part)

    drain(q_ref.at[:, :, pl.ds(0, width)], q_recv.at[0])
    q = head_q(0, 0)
    best = low
    for c in range(KEYS // CHUNK):
        best = scores(0, c, q, sa, best)
    loads[2].wait()

    def step(g, best):
        for b in range(1, QB):
            @pl.when(g == 2 * b - 1)
            def _():
                drain(q_ref.at[:, :, pl.ds(b * width, width)], q_recv.at[b])

        best = attend(g, best)
        send_out(g)

        @pl.when(g >= LAG)
        def _():
            combine(g - LAG)

        @pl.when(g >= 2 * LAG)
        def _():
            project(g - 2 * LAG)

        return best

    lax.fori_loop(0, GROUPS, step, best)
    for g in range(GROUPS - LAG, GROUPS):
        combine(g)
    for g in range(GROUPS - 2 * LAG, GROUPS):
        project(g)

    outs = [
        pltpu.make_async_copy(at_buf.at[kv], att_hbm.at[:, pl.ds(kv * 1024, 1024)], local_sem.at[3 + kv])
        for kv in range(2)
    ]
    for out in outs:
        out.start()
    hd_buf[...] = part[...].astype(jnp.bfloat16)
    copies = []
    for i in (1, 2, 3):
        to = lax.rem(hd + i, 4)
        copies.append(
            remote(
                hd_buf.at[pl.ds(pl.multiple_of(64 * to, 64), 64), :], hd_recv.at[i - 1],
                h_send.at[i - 1], h_rsem.at[i - 1], {"head": to},
            )
        )
        copies[-1].start()
    total = part[pl.ds(pl.multiple_of(64 * hd, 64), 64), :]
    for i in range(3):
        copies[i].wait()
        total = total + hd_recv[i].astype(jnp.float32)
    proj_ref[...] = total.astype(jnp.bfloat16)

    for out in outs:
        out.wait()
    for b in range(QB):
        drain(o_recv.at[pl.ds(0, 1024 // QB // HD), pl.ds(0, HOSTS - 1)], q_send.at[b])
    for g in range(GROUPS):
        drain(o_recv.at[g, pl.ds(0, HOSTS - 1)], o_send.at[g])
        drain(l_recv.at[g, pl.ds(0, HOSTS - 1)], l_send.at[g])
        drain(o_recv.at[g, pl.ds(0, HOSTS - 1)], a_send.at[g])


def attention(qp, keys, values, lengths, w_out):
    vmem = pl.BlockSpec(memory_space=pltpu.VMEM)
    anywhere = pl.BlockSpec(memory_space=pl.ANY)
    bf, f32 = jnp.bfloat16, jnp.float32
    dma = pltpu.SemaphoreType.DMA
    return pl.pallas_call(
        main_kernel,
        out_shape=(jax.ShapeDtypeStruct((ROWS, 2048), bf), jax.ShapeDtypeStruct((64, 256), bf)),
        in_specs=[vmem, anywhere, anywhere, pl.BlockSpec(memory_space=pltpu.SMEM), anywhere],
        out_specs=(anywhere, vmem),
        scratch_shapes=[
            pltpu.VMEM((KEYS, 2, HD), bf), pltpu.VMEM((KEYS, 2, HD), bf), pltpu.VMEM((2048, 256), bf),
            pltpu.VMEM((2, KEYS, HD), bf), pltpu.VMEM((2, HD + 16, KEYS), bf),
            pltpu.VMEM((2, ROWS, 1024), bf),
            pltpu.VMEM((KEYS, ROWS), f32), pltpu.VMEM((KEYS, ROWS), f32),
            pltpu.VMEM((GROUPS, 2, ROWS, HD), bf), pltpu.VMEM((GROUPS, HOSTS, 16, HD), bf),
            pltpu.VMEM((GROUPS, 2, 2, 1, 128), f32), pltpu.VMEM((GROUPS, HOSTS, 1, 128), f32),
            pltpu.VMEM((GROUPS, 16, HD), bf), pltpu.VMEM((2, ROWS, 1024), bf),
            pltpu.VMEM((ROWS, 256), f32), pltpu.VMEM((ROWS, 256), bf), pltpu.VMEM((3, 64, 256), bf),
            dma((5,)), dma((QB,)), dma((QB,)), dma((GROUPS,)), dma((GROUPS,)), dma((GROUPS,)), dma((GROUPS,)),
            dma((GROUPS,)), dma((GROUPS,)), dma((3,)), dma((3,)),
        ],
        compiler_params=pltpu.CompilerParams(
            collective_id=0, has_side_effects=True, vmem_limit_bytes=56 << 20
        ),
    )(qp, keys, values, lengths, w_out)


def body(queries, keys, values, lengths, owner, w_out):
    qp = lax.switch(owner[0], [functools.partial(scatter, o) for o in range(HOSTS)], queries)
    return attention(qp, keys, values, lengths, w_out)


def solution(mesh):
    in_specs = (
        P("ctx", None, "head"),
        P("ctx", "head", None),
        P("ctx", "head", None),
        P("ctx"),
        P(),
        P("head", "ctx"),
    )
    out_specs = (P(None, "head"), P("head", "ctx"))
    return jax.shard_map(body, mesh=mesh, in_specs=in_specs, out_specs=out_specs, check_vma=False)
```

```python
import functools
import math

import jax
import jax.numpy as jnp
from jax import lax
from jax.experimental import pallas as pl
from jax.experimental.pallas import tpu as pltpu
from jax.sharding import PartitionSpec as P

MESH = pl.DeviceIdType.MESH
HOSTS = 32
GROUPS = 8
ROWS = 256
HD = 128
KEYS = 4096
CHUNK = 1024
SCALE = math.log2(math.e) / math.sqrt(HD)
STAGED = 4
AFTER = (0, 2, 4, 6, 8)
QUARTERS = tuple((yy, pl.ds(aa, 2)) for yy in range(2) for aa in (0, 2))
Q_BATCHES = ((0, 2, False), (2, 5, False), (5, 8, True))


def remote(src, dst, send, recv, ctx):
    return pltpu.make_async_remote_copy(
        src_ref=src, dst_ref=dst, send_sem=send, recv_sem=recv, device_id=ctx, device_id_type=MESH
    )


def drain(ref, sem):
    pltpu.make_async_copy(ref, ref, sem).wait()


def scatter_kernel(owner, q_ref, out_ref, send, recv):
    me = lax.axis_index("ctx")
    barrier = pltpu.get_barrier_semaphore()

    @pl.when(me != owner)
    def _():
        pl.semaphore_signal(barrier, inc=1, device_id={"ctx": owner}, device_id_type=MESH)
        drain(out_ref, recv)

    @pl.when(me == owner)
    def _():
        pl.semaphore_wait(barrier, HOSTS - 1)

        def piece(p):
            return q_ref.at[0, pl.ds(16 * (p % 16), 16), pl.ds(1024 * (p // 16), 1024)]

        copies = []
        for step in range(1, HOSTS):
            p = (owner + step) % HOSTS
            copies.append(remote(piece(p), out_ref, send.at[step], recv, {"ctx": p}))
            copies[-1].start()
        own = pltpu.make_async_copy(piece(owner), out_ref, send.at[0])
        own.start()
        own.wait()
        for copy in copies:
            copy.wait_send()


def scatter(owner, queries):
    return pl.pallas_call(
        functools.partial(scatter_kernel, owner),
        out_shape=jax.ShapeDtypeStruct((16, 1024), jnp.bfloat16),
        in_specs=[pl.BlockSpec(memory_space=pl.ANY)],
        out_specs=pl.BlockSpec(memory_space=pltpu.VMEM),
        scratch_shapes=[pltpu.SemaphoreType.DMA((HOSTS,)), pltpu.SemaphoreType.DMA],
        compiler_params=pltpu.CompilerParams(collective_id=owner + 1, has_side_effects=True),
    )(queries)


def main_kernel(
    qp_ref, k_hbm, v_hbm, len_ref, w_hbm, att_hbm, proj_ref,
    k_in, v_in, k_wide, v_wide, eye, w_ref, k_ref, vt_ref, q_ref, sa, sb,
    o_buf, l_buf, r1, l1, s2, l2_buf, r2, l2, d_recv, dl_recv, at_buf, w1, w2, part, hd_buf, hd_recv,
    local_sem, out_sem, q1_send, q1_recv, q2_send, q2_recv, o1_send, o1_recv, l1_send, l1_recv,
    o2_send, o2_recv, l2_send, l2_recv, a1_send, a1_recv, a2_send, a2_recv, h_send, h_recv,
):
    me = lax.axis_index("ctx")
    hd = lax.axis_index("head")
    y, x, z = me // 16, lax.rem(me // 4, 4), lax.rem(me, 4)
    loads = [
        pltpu.make_async_copy(k_hbm, k_in, local_sem.at[0]),
        pltpu.make_async_copy(v_hbm, v_in, local_sem.at[1]),
        pltpu.make_async_copy(w_hbm, w_ref, local_sem.at[2]),
    ]
    for load in loads:
        load.start()
    barrier = pltpu.get_barrier_semaphore()
    for i in range(1, HOSTS):
        pl.semaphore_signal(barrier, inc=1, device_id={"ctx": lax.rem(me + i, HOSTS)}, device_id_type=MESH)
    for i in range(1, 4):
        pl.semaphore_signal(barrier, inc=1, device_id={"head": lax.rem(hd + i, 4)}, device_id_type=MESH)
    pl.semaphore_wait(barrier, HOSTS - 1 + 3)

    def q_cols(b):
        first, last, _ = Q_BATCHES[b]
        return pl.ds(first * HD, (last - first) * HD)

    def q_plane(b):
        cols = q_cols(b)
        return q_ref.at[:, x, :, :, cols] if Q_BATCHES[b][2] else q_ref.at[:, :, z, :, cols]

    for b in range(len(Q_BATCHES)):
        src, dst = qp_ref.at[:, q_cols(b)], q_ref.at[y, x, z, :, q_cols(b)]
        if b == 0:
            for i in range(1, HOSTS):
                remote(src, dst, q1_send.at[b], q1_recv.at[b], {"ctx": lax.rem(me + i, HOSTS)}).start()
        for i in range(1, 8) if b else ():
            if Q_BATCHES[b][2]:
                q = lax.rem(4 * y + z + i, 8)
                to = 16 * (q // 4) + 4 * x + lax.rem(q, 4)
            else:
                q = lax.rem(4 * y + x + i, 8)
                to = 16 * (q // 4) + 4 * lax.rem(q, 4) + z
            remote(src, dst, q1_send.at[b], q1_recv.at[b], {"ctx": to}).start()
        pltpu.make_async_copy(src, dst, q1_recv.at[b]).start()

    def q_ring(b):
        drain(q_plane(b), q1_recv.at[b])
        for i in range(1, 4):
            to = 16 * y + 4 * lax.rem(x + i, 4) + z if Q_BATCHES[b][2] else 16 * y + 4 * x + lax.rem(z + i, 4)
            part_of = q_plane(b)
            for yy, at in QUARTERS:
                own = part_of.at[yy, at]
                remote(own, own, q2_send.at[b], q2_recv.at[b], {"ctx": to}).start()

    def q_ready(b):
        drain(q_ref.at[:, pl.ds(0, 3), :, :, q_cols(b)], q2_recv.at[b])

    count = len_ref[0]
    loads[0].wait()
    for c in range(KEYS // 512):
        at = 512 * c
        k_wide[2 * at : 2 * at + 1024, :] = k_in[2 * at : 2 * at + 1024, :].astype(jnp.float32)
        row = lax.broadcasted_iota(jnp.int32, (512, HD), 0) + at
        for kv in range(2):
            k_ref[kv, at : at + 512, :] = jnp.where(
                row < count, k_wide[pl.ds(2 * at + kv, 512, stride=2), :], k_wide[kv : kv + 1, :]
            ).astype(jnp.bfloat16)
    loads[1].wait()
    eye[...] = jnp.where(
        lax.broadcasted_iota(jnp.int32, (HD, HD), 0) == lax.broadcasted_iota(jnp.int32, (HD, HD), 1), 1.0, 0.0
    ).astype(jnp.bfloat16)
    for c in range(KEYS // 512):
        at = 512 * c
        v_wide[2 * at : 2 * at + 1024, :] = v_in[2 * at : 2 * at + 1024, :].astype(jnp.float32)
        row = lax.broadcasted_iota(jnp.int32, (512, HD), 0) + at
        col = lax.broadcasted_iota(jnp.int32, (16, 512), 1) + at
        for kv in range(2):
            v = jnp.where(row < count, v_wide[pl.ds(2 * at + kv, 512, stride=2), :], 0.0).astype(jnp.bfloat16)
            vt_ref[kv, 0:HD, at : at + 512] = lax.dot_general(
                eye[...], v, (((1,), (1,)), ((), ())), preferred_element_type=jnp.float32
            ).astype(jnp.bfloat16)
            vt_ref[kv, HD : HD + 16, at : at + 512] = jnp.where(col < count, 1.0, 0.0).astype(jnp.bfloat16)
    for b in range(1, len(Q_BATCHES)):
        q_ring(b)

    def head_q(g, kv):
        return q_ref[kv, :, :, :, pl.ds(pl.multiple_of(g * HD, HD), HD)].reshape(ROWS, HD)

    def scores(kv, c, q, s_ref, top):
        at = c * CHUNK
        s = lax.dot_general(
            k_ref[kv, at : at + CHUNK, :], q, (((1,), (1,)), ((), ())), preferred_element_type=jnp.float32
        )
        s_ref[at : at + CHUNK, :] = s
        return jnp.maximum(top, jnp.max(s.reshape(CHUNK // 8, 8, ROWS), axis=0))

    def weigh(kv, c, s_ref, top, acc):
        at = c * CHUNK
        p = jnp.exp2(s_ref[at : at + CHUNK, :] * SCALE - top).astype(jnp.bfloat16)
        return acc + jnp.dot(vt_ref[kv, 0 : HD + 8, at : at + CHUNK], p, preferred_element_type=jnp.float32)

    def finish(g, kv, acc, top):
        total = acc[HD : HD + 1]
        o_buf[g, kv] = (acc[:HD] / total).T.astype(jnp.bfloat16).reshape(4, 4, 16, HD)
        lse = top + jnp.log2(total)
        l_buf[g, 2 * kv] = lse[:, :128]
        l_buf[g, 2 * kv + 1] = lse[:, 128:]

    low = jnp.full((8, ROWS), -jnp.inf, jnp.float32)
    zero = jnp.zeros((HD + 8, ROWS), jnp.float32)

    def attend(g, best):
        top = jnp.max(best, axis=0, keepdims=True) * SCALE
        q = head_q(g, 1)
        other, acc = low, zero
        for c in range(KEYS // CHUNK):
            other = scores(1, c, q, sb, other)
            acc = weigh(0, c, sa, top, acc)
        finish(g, 0, acc, top)
        top = jnp.max(other, axis=0, keepdims=True) * SCALE
        q = head_q(jnp.minimum(g + 1, GROUPS - 1), 0)
        best, acc = low, zero
        for c in range(KEYS // CHUNK):
            best = scores(0, c, q, sa, best)
            acc = weigh(1, c, sb, top, acc)
        finish(g, 1, acc, top)
        return best

    def place(g):
        odd = lax.rem(g, 2)
        a, b = x + odd * (z - x), z + odd * (x - z)

        def host(yy, aa, bb):
            return {"ctx": 16 * yy + (4 - 3 * odd) * aa + (1 + 3 * odd) * bb}

        return a, b, host

    def plane(g):
        a, b, host = place(g)
        for i in range(1, 8):
            q = lax.rem(4 * y + a + i, 8)
            yield q // 4, lax.rem(q, 4), host(q // 4, lax.rem(q, 4), b)

    def ring(g):
        a, b, host = place(g)
        for i in range(1, 4):
            bb = lax.rem(b + i, 4)
            yield bb, host(y, a, bb)

    def send_ring(g):
        a, b, _ = place(g)
        for bb, to in ring(g):
            remote(l_buf.at[g], l1.at[g, b], l1_send.at[g], l1_recv.at[g], to).start()
            for yy, at in QUARTERS:
                remote(
                    o_buf.at[g, yy, at, bb], r1.at[g, b, yy, at], o1_send.at[g], o1_recv.at[g], to
                ).start()
        pltpu.make_async_copy(l_buf.at[g], l1.at[g, b], l1_recv.at[g]).start()
        pltpu.make_async_copy(o_buf.at[g, :, :, b], r1.at[g, b], o1_recv.at[g]).start()

    def combine_ring(g):
        a, b, _ = place(g)
        drain(l1.at[g], l1_recv.at[g])
        lse = l1[g, :, :, 0, :]
        top = jnp.max(lse, axis=0)
        w = jnp.exp2(lse - top[None])
        total = jnp.sum(w, axis=0)
        w = (w / total[None]).reshape(16, 128)
        w1[...] = jnp.concatenate([w, jnp.zeros((112, 128), jnp.float32)], 0).T
        l2_buf[g, :, 0, :] = top + jnp.log2(total)
        drain(r1.at[g], o1_recv.at[g])
        for aa in range(4):
            ws = w1[pl.ds(pl.multiple_of(64 * (aa % 2) + 16 * b, 16), 16), :]
            for yy in range(2):
                acc = jnp.zeros((16, HD), jnp.float32)
                for src in range(4):
                    at = 4 * src + 2 * yy + aa // 2
                    acc = acc + ws[:, at : at + 1] * r1[g, src, yy, aa].astype(jnp.float32)
                s2[g, yy, aa] = acc.astype(jnp.bfloat16)
        mine = 4 * y + a
        for yy, aa, to in plane(g):
            remote(l2_buf.at[g, 2 * yy + aa // 2], l2.at[g, mine], l2_send.at[g], l2_recv.at[g], to).start()
            remote(s2.at[g, yy, aa], r2.at[g, mine], o2_send.at[g], o2_recv.at[g], to).start()
        pltpu.make_async_copy(l2_buf.at[g, 2 * y + a // 2], l2.at[g, mine], l2_recv.at[g]).start()
        pltpu.make_async_copy(s2.at[g, y, a], r2.at[g, mine], o2_recv.at[g]).start()

    def combine_plane(g):
        a, b, _ = place(g)
        drain(l2.at[g], l2_recv.at[g])
        lse = l2[g, :, 0, :]
        w = jnp.exp2(lse - jnp.max(lse, axis=0, keepdims=True))
        w = w / jnp.sum(w, axis=0, keepdims=True)
        w2[...] = jnp.concatenate([w, jnp.zeros((120, 128), jnp.float32)], 0).T
        drain(r2.at[g], o2_recv.at[g])
        ws = w2[pl.ds(pl.multiple_of(64 * lax.rem(a, 2) + 16 * b, 16), 16), :]
        acc = jnp.zeros((16, HD), jnp.float32)
        for src in range(8):
            acc = acc + ws[:, src : src + 1] * r2[g, src].astype(jnp.float32)
        at_buf[g, y, a, b] = acc.astype(jnp.bfloat16)
        own = at_buf.at[g, y, a, b]
        for _, _, to in plane(g):
            remote(own, own, a1_send.at[g], a1_recv.at[g], to).start()

    def gather_ring(g):
        a, b, _ = place(g)
        drain(r2.at[g, pl.ds(0, 7)], a1_recv.at[g])
        for _, to in ring(g):
            for yy, at in QUARTERS:
                own = at_buf.at[g, yy, at, b]
                remote(own, own, a2_send.at[g], a2_recv.at[g], to).start()

    def result(g, kv):
        return pltpu.make_async_copy(
            at_buf.at[g, kv], att_hbm.at[:, :, :, pl.ds(pl.multiple_of(kv * 1024 + g * HD, HD), HD)], out_sem.at[g]
        )

    def project(g):
        drain(r1.at[g, pl.ds(0, 3)], a2_recv.at[g])
        multiply(g)

    def multiply(g):
        for kv in range(2):
            result(g, kv).start()
            rows = pl.ds(pl.multiple_of(kv * 1024 + g * HD, HD), HD)
            part[...] += jnp.dot(
                at_buf[g, kv].reshape(ROWS, HD), w_ref[rows, :], preferred_element_type=jnp.float32
            )

    stages = (send_ring, combine_ring, combine_plane, gather_ring, project)

    def send_direct(g):
        j = g - STAGED
        for i in range(1, HOSTS):
            p = lax.rem(me + i, HOSTS)
            aa, bb = lax.rem(p // 4, 4), lax.rem(p, 4)
            remote(l_buf.at[g, p // 8], dl_recv.at[j, me], l1_send.at[g], l1_recv.at[g], {"ctx": p}).start()
            remote(o_buf.at[g, p // 16, aa, bb], d_recv.at[j, me], o1_send.at[g], o1_recv.at[g], {"ctx": p}).start()
        pltpu.make_async_copy(l_buf.at[g, me // 8], dl_recv.at[j, me], l1_recv.at[g]).start()
        pltpu.make_async_copy(o_buf.at[g, y, x, z], d_recv.at[j, me], o1_recv.at[g]).start()

    def combine_direct(g):
        j = g - STAGED
        drain(dl_recv.at[j], l1_recv.at[g])
        lse = dl_recv[j, :, 0, :]
        w = jnp.exp2(lse - jnp.max(lse, axis=0, keepdims=True))
        w = w / jnp.sum(w, axis=0, keepdims=True)
        w2[...] = jnp.concatenate([w, jnp.zeros((96, 128), jnp.float32)], 0).T
        drain(d_recv.at[j], o1_recv.at[g])
        ws = w2[pl.ds(pl.multiple_of(64 * lax.rem(x, 2) + 16 * z, 16), 16), :]
        acc = jnp.zeros((16, HD), jnp.float32)
        for src in range(HOSTS):
            acc = acc + ws[:, src : src + 1] * d_recv[j, src].astype(jnp.float32)
        at_buf[g, y, x, z] = acc.astype(jnp.bfloat16)
        own = at_buf.at[g, y, x, z]
        for i in range(1, HOSTS):
            remote(own, own, a1_send.at[g], a1_recv.at[g], {"ctx": lax.rem(me + i, HOSTS)}).start()

    def project_direct(g):
        drain(d_recv.at[g - STAGED, pl.ds(0, HOSTS - 1)], a1_recv.at[g])
        multiply(g)

    def exchange(g):
        for n in reversed(range(len(stages))):
            @pl.when((g >= AFTER[n]) & (g < STAGED + AFTER[n]))
            def _():
                stages[n](g - AFTER[n])

    part[...] = jnp.zeros_like(part)
    drain(q_ref.at[:, :, :, :, q_cols(0)], q1_recv.at[0])
    q = head_q(0, 0)
    best = low
    for c in range(KEYS // CHUNK):
        best = scores(0, c, q, sa, best)
    loads[2].wait()

    def step(g, best):
        for b in range(1, len(Q_BATCHES)):
            @pl.when(g == Q_BATCHES[b][0] - 1)
            def _():
                q_ready(b)

        best = attend(g, best)

        @pl.when(g >= STAGED)
        def _():
            send_direct(g)

        @pl.when(g >= STAGED + 2)
        def _():
            combine_direct(g - 2)

        exchange(g)
        return best

    lax.fori_loop(0, GROUPS, step, best)

    if STAGED <= GROUPS - 2:
        combine_direct(GROUPS - 2)
    for n in range(1, len(stages)):
        for g in range(STAGED):
            if GROUPS <= g + AFTER[n]:
                stages[n](g)
        if n == 1 and STAGED < GROUPS:
            combine_direct(GROUPS - 1)
    for g in range(STAGED, GROUPS):
        project_direct(g)

    hd_buf[...] = part[...].astype(jnp.bfloat16)
    for i in (1, 2, 3):
        to = lax.rem(hd + i, 4)
        for n in range(4):
            remote(
                hd_buf.at[pl.ds(pl.multiple_of(64 * to + 16 * n, 16), 16), :], hd_recv.at[i - 1, pl.ds(16 * n, 16)],
                h_send.at[i - 1], h_recv.at[i - 1], {"head": to},
            ).start()
    total = part[pl.ds(pl.multiple_of(64 * hd, 64), 64), :]
    for i in range(3):
        drain(hd_recv.at[i], h_recv.at[i])
        total = total + hd_recv[i].astype(jnp.float32)
    proj_ref[...] = total.astype(jnp.bfloat16)

    for b in range(len(Q_BATCHES)):
        n = Q_BATCHES[b][1] - Q_BATCHES[b][0]
        if b == 0:
            drain(o_buf.at[pl.ds(0, 2), 0, pl.ds(0, 3)], q1_send.at[b])
            drain(r2.at[pl.ds(0, 2), pl.ds(0, 7)], q1_send.at[b])
            drain(r2.at[pl.ds(0, 2), pl.ds(0, 6)], q1_send.at[b])
            drain(r2.at[pl.ds(0, 2), pl.ds(0, 6)], q1_send.at[b])
        else:
            drain(r2.at[pl.ds(0, n), pl.ds(0, 7)], q1_send.at[b])
            drain(q_ref.at[:, pl.ds(0, 3), :, :, q_cols(b)], q2_send.at[b])

    for g in range(STAGED):
        drain(r1.at[g, pl.ds(0, 3)], o1_send.at[g])
        drain(l1.at[g, pl.ds(0, 3)], l1_send.at[g])
        drain(r2.at[g, pl.ds(0, 7)], o2_send.at[g])
        drain(l2.at[g, pl.ds(0, 7)], l2_send.at[g])
        drain(r2.at[g, pl.ds(0, 7)], a1_send.at[g])
        drain(r1.at[g, pl.ds(0, 3)], a2_send.at[g])
    for j in range(GROUPS - STAGED):
        drain(d_recv.at[j, pl.ds(0, HOSTS - 1)], o1_send.at[STAGED + j])
        drain(dl_recv.at[j, pl.ds(0, HOSTS - 1)], l1_send.at[STAGED + j])
        drain(d_recv.at[j, pl.ds(0, HOSTS - 1)], a1_send.at[STAGED + j])
    for g in range(GROUPS):
        for kv in range(2):
            result(g, kv).wait()
    for i in range(3):
        drain(hd_recv.at[i], h_send.at[i])


def attention(qp, keys, values, lengths, w_out):
    vmem = pl.BlockSpec(memory_space=pltpu.VMEM)
    anywhere = pl.BlockSpec(memory_space=pl.ANY)
    bf, f32 = jnp.bfloat16, jnp.float32
    dma = pltpu.SemaphoreType.DMA
    nq, n = len(Q_BATCHES), GROUPS
    scratch = [
        ((2 * KEYS, HD), bf), ((2 * KEYS, HD), bf), ((2 * KEYS, HD), f32), ((2 * KEYS, HD), f32), ((HD, HD), bf),
        ((2048, 256), bf), ((2, KEYS, HD), bf), ((2, HD + 16, KEYS), bf), ((2, 4, 4, 16, 1024), bf),
        ((KEYS, ROWS), f32), ((KEYS, ROWS), f32),
        ((n, 2, 4, 4, 16, HD), bf), ((n, 4, 1, 128), f32), ((n, 4, 2, 4, 16, HD), bf), ((n, 4, 4, 1, 128), f32),
        ((n, 2, 4, 16, HD), bf), ((n, 4, 1, 128), f32), ((n, 8, 16, HD), bf), ((n, 8, 1, 128), f32),
        ((n - STAGED, HOSTS, 16, HD), bf), ((n - STAGED, HOSTS, 1, 128), f32),
        ((n, 2, 4, 4, 16, HD), bf), ((128, 128), f32), ((128, 128), f32),
        ((ROWS, 256), f32), ((ROWS, 256), bf), ((3, 64, 256), bf),
    ]
    sems = [3, n, nq, nq, nq, nq] + [n] * 12 + [3, 3]
    att, proj = pl.pallas_call(
        main_kernel,
        out_shape=(jax.ShapeDtypeStruct((4, 4, 16, 2048), bf), jax.ShapeDtypeStruct((64, 256), bf)),
        in_specs=[vmem, anywhere, anywhere, pl.BlockSpec(memory_space=pltpu.SMEM), anywhere],
        out_specs=(anywhere, vmem),
        scratch_shapes=[pltpu.VMEM(*s) for s in scratch] + [dma((k,)) for k in sems],
        compiler_params=pltpu.CompilerParams(
            collective_id=0, has_side_effects=True, vmem_limit_bytes=56 << 20
        ),
    )(qp, keys.reshape(2 * KEYS, HD), values.reshape(2 * KEYS, HD), lengths, w_out)
    return settle(att.reshape(ROWS, 2048), proj)


def settle_kernel(att_ref, proj_ref, att_out, proj_out):
    att_out[...] = att_ref[...]
    proj_out[...] = proj_ref[...]


def settle(att, proj):
    vmem = pl.BlockSpec(memory_space=pltpu.VMEM)
    return pl.pallas_call(
        settle_kernel,
        out_shape=(jax.ShapeDtypeStruct(att.shape, att.dtype), jax.ShapeDtypeStruct(proj.shape, proj.dtype)),
        in_specs=[vmem, vmem],
        out_specs=(vmem, vmem),
    )(att, proj)


def body(queries, keys, values, lengths, owner, w_out):
    qp = lax.switch(owner[0], [functools.partial(scatter, o) for o in range(HOSTS)], queries)
    return attention(qp, keys, values, lengths, w_out)


def solution(mesh):
    in_specs = (
        P("ctx", None, "head"),
        P("ctx", "head", None),
        P("ctx", "head", None),
        P("ctx"),
        P(),
        P("head", "ctx"),
    )
    out_specs = (P(None, "head"), P("head", "ctx"))
    return jax.shard_map(body, mesh=mesh, in_specs=in_specs, out_specs=out_specs, check_vma=False)
```

```python
import functools
import math

import jax
import jax.numpy as jnp
from jax import lax
from jax.experimental import pallas as pl
from jax.experimental.pallas import tpu as pltpu
from jax.sharding import PartitionSpec as P

MESH = pl.DeviceIdType.MESH
HOSTS = 32
GROUPS = 8
ROWS = 256
HD = 128
KEYS = 4096
CHUNK = 1024
SCALE = math.log2(math.e) / math.sqrt(HD)
STAGED = 4
AFTER = (0, 2, 4, 6, 8)
OTHERS = sorted(
    ((dy, dx, dz) for dy in range(2) for dx in range(4) for dz in range(4) if (dy, dx, dz) != (0, 0, 0)),
    key=lambda d: -(2 * d[0] + min(d[1], 4 - d[1]) + min(d[2], 4 - d[2])),
)
Q_BATCHES = ((0, 2, False), (2, 5, False), (5, 8, True))


def remote(src, dst, send, recv, ctx):
    return pltpu.make_async_remote_copy(
        src_ref=src, dst_ref=dst, send_sem=send, recv_sem=recv, device_id=ctx, device_id_type=MESH
    )


def drain(ref, sem):
    pltpu.make_async_copy(ref, ref, sem).wait()


def scatter_kernel(owner, q_ref, out_ref, send, recv):
    me = lax.axis_index("ctx")
    barrier = pltpu.get_barrier_semaphore()

    @pl.when(me != owner)
    def _():
        pl.semaphore_signal(barrier, inc=1, device_id={"ctx": owner}, device_id_type=MESH)
        drain(out_ref, recv)

    @pl.when(me == owner)
    def _():
        pl.semaphore_wait(barrier, HOSTS - 1)

        def piece(p):
            return q_ref.at[0, pl.ds(16 * (p % 16), 16), pl.ds(1024 * (p // 16), 1024)]

        copies = []
        for step, (dy, dx, dz) in enumerate(OTHERS, 1):
            p = 16 * ((owner // 16 + dy) % 2) + 4 * ((owner // 4 + dx) % 4) + (owner + dz) % 4
            copies.append(remote(piece(p), out_ref, send.at[step], recv, {"ctx": p}))
            copies[-1].start()
        own = pltpu.make_async_copy(piece(owner), out_ref, send.at[0])
        own.start()
        own.wait()
        for copy in copies:
            copy.wait_send()


def scatter(owner, queries):
    return pl.pallas_call(
        functools.partial(scatter_kernel, owner),
        out_shape=jax.ShapeDtypeStruct((16, 1024), jnp.bfloat16),
        in_specs=[pl.BlockSpec(memory_space=pl.ANY)],
        out_specs=pl.BlockSpec(memory_space=pltpu.VMEM),
        scratch_shapes=[pltpu.SemaphoreType.DMA((HOSTS,)), pltpu.SemaphoreType.DMA],
        compiler_params=pltpu.CompilerParams(collective_id=owner + 1, has_side_effects=True),
    )(queries)


def main_kernel(
    qp_ref, k_hbm, v_hbm, len_ref, w_hbm, att_hbm, proj_ref,
    k_in, v_in, k_wide, v_wide, eye, w_ref, k_ref, vt_ref, q_ref, sa, sb,
    o_buf, l_buf, r1, l1, s2, l2_buf, r2, l2, d_recv, dl_recv, at_buf, w1, w2, part, hd_buf, hd_recv,
    local_sem, out_sem, q1_send, q1_recv, q2_send, q2_recv, o1_send, o1_recv, l1_send, l1_recv,
    o2_send, o2_recv, l2_send, l2_recv, a1_send, a1_recv, a2_send, a2_recv, h_send, h_recv,
):
    me = lax.axis_index("ctx")
    hd = lax.axis_index("head")
    y, x, z = me // 16, lax.rem(me // 4, 4), lax.rem(me, 4)
    loads = [
        pltpu.make_async_copy(k_hbm, k_in, local_sem.at[0]),
        pltpu.make_async_copy(v_hbm, v_in, local_sem.at[1]),
        pltpu.make_async_copy(w_hbm, w_ref, local_sem.at[2]),
    ]
    for load in loads:
        load.start()
    barrier = pltpu.get_barrier_semaphore()
    for i in range(1, HOSTS):
        pl.semaphore_signal(barrier, inc=1, device_id={"ctx": lax.rem(me + i, HOSTS)}, device_id_type=MESH)
    for i in range(1, 4):
        pl.semaphore_signal(barrier, inc=1, device_id={"head": lax.rem(hd + i, 4)}, device_id_type=MESH)
    count = len_ref[0]
    loads[0].wait()
    for c in range(KEYS // 512):
        at = 512 * c
        k_wide[2 * at : 2 * at + 1024, :] = k_in[2 * at : 2 * at + 1024, :].astype(jnp.float32)
        row = lax.broadcasted_iota(jnp.int32, (512, HD), 0) + at
        for kv in range(2):
            k_ref[kv, at : at + 512, :] = jnp.where(
                row < count, k_wide[pl.ds(2 * at + kv, 512, stride=2), :], k_wide[kv : kv + 1, :]
            ).astype(jnp.bfloat16)
    pl.semaphore_wait(barrier, HOSTS - 1 + 3)

    def others():
        for dy, dx, dz in OTHERS:
            yield lax.rem(y + dy, 2), lax.rem(x + dx, 4), lax.rem(z + dz, 4)

    def q_cols(b):
        first, last, _ = Q_BATCHES[b]
        return pl.ds(first * HD, (last - first) * HD)

    def q_plane(b):
        cols = q_cols(b)
        return q_ref.at[:, x, :, :, cols] if Q_BATCHES[b][2] else q_ref.at[:, :, z, :, cols]

    for b in range(len(Q_BATCHES)):
        src, dst = qp_ref.at[:, q_cols(b)], q_ref.at[y, x, z, :, q_cols(b)]
        if b == 0:
            for yy, xx, zz in others():
                remote(src, dst, q1_send.at[b], q1_recv.at[b], {"ctx": 16 * yy + 4 * xx + zz}).start()
        for i in range(1, 8) if b else ():
            if Q_BATCHES[b][2]:
                q = lax.rem(4 * y + z + i, 8)
                to = 16 * (q // 4) + 4 * x + lax.rem(q, 4)
            else:
                q = lax.rem(4 * y + x + i, 8)
                to = 16 * (q // 4) + 4 * lax.rem(q, 4) + z
            remote(src, dst, q1_send.at[b], q1_recv.at[b], {"ctx": to}).start()
        pltpu.make_async_copy(src, dst, q1_recv.at[b]).start()

    def q_ring(b):
        drain(q_plane(b), q1_recv.at[b])
        for i in range(1, 4):
            to = 16 * y + 4 * lax.rem(x + i, 4) + z if Q_BATCHES[b][2] else 16 * y + 4 * x + lax.rem(z + i, 4)
            remote(q_plane(b), q_plane(b), q2_send.at[b], q2_recv.at[b], {"ctx": to}).start()

    def q_ready(b):
        drain(q_ref.at[:, pl.ds(0, 3), :, :, q_cols(b)], q2_recv.at[b])

    loads[1].wait()
    eye[...] = jnp.where(
        lax.broadcasted_iota(jnp.int32, (HD, HD), 0) == lax.broadcasted_iota(jnp.int32, (HD, HD), 1), 1.0, 0.0
    ).astype(jnp.bfloat16)
    for c in range(KEYS // 512):
        at = 512 * c
        v_wide[2 * at : 2 * at + 1024, :] = v_in[2 * at : 2 * at + 1024, :].astype(jnp.float32)
        row = lax.broadcasted_iota(jnp.int32, (512, HD), 0) + at
        col = lax.broadcasted_iota(jnp.int32, (16, 512), 1) + at
        for kv in range(2):
            v = jnp.where(row < count, v_wide[pl.ds(2 * at + kv, 512, stride=2), :], 0.0).astype(jnp.bfloat16)
            vt_ref[kv, 0:HD, at : at + 512] = lax.dot_general(
                eye[...], v, (((1,), (1,)), ((), ())), preferred_element_type=jnp.float32
            ).astype(jnp.bfloat16)
            vt_ref[kv, HD : HD + 16, at : at + 512] = jnp.where(col < count, 1.0, 0.0).astype(jnp.bfloat16)
    for b in range(1, len(Q_BATCHES)):
        q_ring(b)

    def head_q(g, kv):
        return q_ref[kv, :, :, :, pl.ds(pl.multiple_of(g * HD, HD), HD)].reshape(ROWS, HD)

    def scores(kv, c, q, s_ref, top):
        at = c * CHUNK
        s = lax.dot_general(
            k_ref[kv, at : at + CHUNK, :], q, (((1,), (1,)), ((), ())), preferred_element_type=jnp.float32
        )
        s_ref[at : at + CHUNK, :] = s
        return jnp.maximum(top, jnp.max(s.reshape(CHUNK // 8, 8, ROWS), axis=0))

    def weigh(kv, c, s_ref, top, acc):
        at = c * CHUNK
        p = jnp.exp2(s_ref[at : at + CHUNK, :] * SCALE - top).astype(jnp.bfloat16)
        return acc + jnp.dot(vt_ref[kv, 0 : HD + 8, at : at + CHUNK], p, preferred_element_type=jnp.float32)

    def finish(g, kv, acc, top):
        total = acc[HD : HD + 1]
        o_buf[g, kv] = (acc[:HD] * (1.0 / total)).astype(jnp.bfloat16).T.reshape(4, 4, 16, HD)
        lse = top + jnp.log2(total)
        l_buf[g, 2 * kv] = lse[:, :128]
        l_buf[g, 2 * kv + 1] = lse[:, 128:]

    low = jnp.full((8, ROWS), -jnp.inf, jnp.float32)
    zero = jnp.zeros((HD + 8, ROWS), jnp.float32)

    def attend(g, best):
        top = jnp.max(best, axis=0, keepdims=True) * SCALE
        q = head_q(g, 1)
        other, acc = low, zero
        for c in range(KEYS // CHUNK):
            other = scores(1, c, q, sb, other)
            acc = weigh(0, c, sa, top, acc)
        finish(g, 0, acc, top)
        top = jnp.max(other, axis=0, keepdims=True) * SCALE
        q = head_q(jnp.minimum(g + 1, GROUPS - 1), 0)
        best, acc = low, zero
        for c in range(KEYS // CHUNK):
            best = scores(0, c, q, sa, best)
            acc = weigh(1, c, sb, top, acc)
        finish(g, 1, acc, top)
        return best

    def place(g):
        odd = lax.rem(g, 2)
        a, b = x + odd * (z - x), z + odd * (x - z)

        def host(yy, aa, bb):
            return {"ctx": 16 * yy + (4 - 3 * odd) * aa + (1 + 3 * odd) * bb}

        return a, b, host

    def plane(g):
        a, b, host = place(g)
        for i in range(1, 8):
            q = lax.rem(4 * y + a + i, 8)
            yield q // 4, lax.rem(q, 4), host(q // 4, lax.rem(q, 4), b)

    def ring(g):
        a, b, host = place(g)
        for i in range(1, 4):
            bb = lax.rem(b + i, 4)
            yield bb, host(y, a, bb)

    def send_ring(g):
        a, b, _ = place(g)
        for bb, to in ring(g):
            remote(l_buf.at[g], l1.at[g, b], l1_send.at[g], l1_recv.at[g], to).start()
            remote(o_buf.at[g, :, :, bb], r1.at[g, b], o1_send.at[g], o1_recv.at[g], to).start()
        pltpu.make_async_copy(l_buf.at[g], l1.at[g, b], l1_recv.at[g]).start()
        pltpu.make_async_copy(o_buf.at[g, :, :, b], r1.at[g, b], o1_recv.at[g]).start()

    def combine_ring(g):
        a, b, _ = place(g)
        drain(l1.at[g], l1_recv.at[g])
        lse = l1[g, :, :, 0, :]
        top = jnp.max(lse, axis=0)
        w = jnp.exp2(lse - top[None])
        total = jnp.sum(w, axis=0)
        w = (w / total[None]).reshape(16, 128)
        w1[...] = jnp.concatenate([w, jnp.zeros((112, 128), jnp.float32)], 0).T
        l2_buf[g, :, 0, :] = top + jnp.log2(total)
        drain(r1.at[g], o1_recv.at[g])
        for aa in range(4):
            ws = w1[pl.ds(pl.multiple_of(64 * (aa % 2) + 16 * b, 16), 16), :]
            for yy in range(2):
                acc = jnp.zeros((16, HD), jnp.float32)
                for src in range(4):
                    at = 4 * src + 2 * yy + aa // 2
                    acc = acc + ws[:, at : at + 1] * r1[g, src, yy, aa].astype(jnp.float32)
                s2[g, yy, aa] = acc.astype(jnp.bfloat16)
        mine = 4 * y + a
        for yy, aa, to in plane(g):
            remote(l2_buf.at[g, 2 * yy + aa // 2], l2.at[g, mine], l2_send.at[g], l2_recv.at[g], to).start()
            remote(s2.at[g, yy, aa], r2.at[g, mine], o2_send.at[g], o2_recv.at[g], to).start()
        pltpu.make_async_copy(l2_buf.at[g, 2 * y + a // 2], l2.at[g, mine], l2_recv.at[g]).start()
        pltpu.make_async_copy(s2.at[g, y, a], r2.at[g, mine], o2_recv.at[g]).start()

    def combine_plane(g):
        a, b, _ = place(g)
        drain(l2.at[g], l2_recv.at[g])
        lse = l2[g, :, 0, :]
        w = jnp.exp2(lse - jnp.max(lse, axis=0, keepdims=True))
        w = w / jnp.sum(w, axis=0, keepdims=True)
        w2[...] = jnp.concatenate([w, jnp.zeros((120, 128), jnp.float32)], 0).T
        drain(r2.at[g], o2_recv.at[g])
        ws = w2[pl.ds(pl.multiple_of(64 * lax.rem(a, 2) + 16 * b, 16), 16), :]
        acc = jnp.zeros((16, HD), jnp.float32)
        for src in range(8):
            acc = acc + ws[:, src : src + 1] * r2[g, src].astype(jnp.float32)
        at_buf[g, y, a, b] = acc.astype(jnp.bfloat16)
        own = at_buf.at[g, y, a, b]
        for _, _, to in plane(g):
            remote(own, own, a1_send.at[g], a1_recv.at[g], to).start()

    def gather_ring(g):
        a, b, _ = place(g)
        drain(r2.at[g, pl.ds(0, 7)], a1_recv.at[g])
        for _, to in ring(g):
            own = at_buf.at[g, :, :, b]
            remote(own, own, a2_send.at[g], a2_recv.at[g], to).start()

    def result(g, kv):
        return pltpu.make_async_copy(
            at_buf.at[g, kv], att_hbm.at[:, :, :, pl.ds(pl.multiple_of(kv * 1024 + g * HD, HD), HD)], out_sem.at[g]
        )

    def project(g):
        drain(r1.at[g, pl.ds(0, 3)], a2_recv.at[g])
        multiply(g)

    def multiply(g):
        for kv in range(2):
            result(g, kv).start()
            rows = pl.ds(pl.multiple_of(kv * 1024 + g * HD, HD), HD)
            part[...] += jnp.dot(
                at_buf[g, kv].reshape(ROWS, HD), w_ref[rows, :], preferred_element_type=jnp.float32
            )

    stages = (send_ring, combine_ring, combine_plane, gather_ring, project)

    def send_direct(g):
        j = g - STAGED
        for yy, xx, zz in others():
            p = {"ctx": 16 * yy + 4 * xx + zz}
            remote(l_buf.at[g, 2 * yy + xx // 2], dl_recv.at[j, me], l1_send.at[g], l1_recv.at[g], p).start()
            remote(o_buf.at[g, yy, xx, zz], d_recv.at[j, me], o1_send.at[g], o1_recv.at[g], p).start()
        pltpu.make_async_copy(l_buf.at[g, me // 8], dl_recv.at[j, me], l1_recv.at[g]).start()
        pltpu.make_async_copy(o_buf.at[g, y, x, z], d_recv.at[j, me], o1_recv.at[g]).start()

    def combine_direct(g):
        j = g - STAGED
        drain(dl_recv.at[j], l1_recv.at[g])
        lse = dl_recv[j, :, 0, :]
        w = jnp.exp2(lse - jnp.max(lse, axis=0, keepdims=True))
        w = w / jnp.sum(w, axis=0, keepdims=True)
        w2[...] = jnp.concatenate([w, jnp.zeros((96, 128), jnp.float32)], 0).T
        drain(d_recv.at[j], o1_recv.at[g])
        ws = w2[pl.ds(pl.multiple_of(64 * lax.rem(x, 2) + 16 * z, 16), 16), :]
        acc = jnp.zeros((16, HD), jnp.float32)
        for src in range(HOSTS):
            acc = acc + ws[:, src : src + 1] * d_recv[j, src].astype(jnp.float32)
        at_buf[g, y, x, z] = acc.astype(jnp.bfloat16)
        own = at_buf.at[g, y, x, z]
        for yy, xx, zz in others():
            remote(own, own, a1_send.at[g], a1_recv.at[g], {"ctx": 16 * yy + 4 * xx + zz}).start()

    def project_direct(g):
        drain(d_recv.at[g - STAGED, pl.ds(0, HOSTS - 1)], a1_recv.at[g])
        multiply(g)

    def exchange(g):
        for n in reversed(range(len(stages))):
            @pl.when((g >= AFTER[n]) & (g < STAGED + AFTER[n]))
            def _():
                stages[n](g - AFTER[n])

    part[...] = jnp.zeros_like(part)
    drain(q_ref.at[:, :, :, :, q_cols(0)], q1_recv.at[0])
    q = head_q(0, 0)
    best = low
    for c in range(KEYS // CHUNK):
        best = scores(0, c, q, sa, best)
    loads[2].wait()

    def step(g, best):
        for b in range(1, len(Q_BATCHES)):
            @pl.when(g == Q_BATCHES[b][0] - 1)
            def _():
                q_ready(b)

        best = attend(g, best)

        @pl.when(g >= STAGED)
        def _():
            send_direct(g)

        @pl.when(g >= STAGED + 2)
        def _():
            combine_direct(g - 2)

        exchange(g)
        return best

    lax.fori_loop(0, GROUPS, step, best)

    if STAGED <= GROUPS - 2:
        combine_direct(GROUPS - 2)
    for n in range(1, len(stages)):
        for g in range(STAGED):
            if GROUPS <= g + AFTER[n]:
                stages[n](g)
        if n == 1 and STAGED < GROUPS:
            combine_direct(GROUPS - 1)
    for g in range(STAGED, GROUPS):
        project_direct(g)

    hd_buf[...] = part[...].astype(jnp.bfloat16)
    for i in (1, 2, 3):
        to = lax.rem(hd + i, 4)
        for n in range(4):
            remote(
                hd_buf.at[pl.ds(pl.multiple_of(64 * to + 16 * n, 16), 16), :], hd_recv.at[i - 1, pl.ds(16 * n, 16)],
                h_send.at[i - 1], h_recv.at[i - 1], {"head": to},
            ).start()
    total = part[pl.ds(pl.multiple_of(64 * hd, 64), 64), :]
    for i in range(3):
        drain(hd_recv.at[i], h_recv.at[i])
        total = total + hd_recv[i].astype(jnp.float32)
    proj_ref[...] = total.astype(jnp.bfloat16)

    for b in range(len(Q_BATCHES)):
        n = Q_BATCHES[b][1] - Q_BATCHES[b][0]
        if b == 0:
            drain(o_buf.at[pl.ds(0, 2), 0, pl.ds(0, 3)], q1_send.at[b])
            drain(r2.at[pl.ds(0, 2), pl.ds(0, 7)], q1_send.at[b])
            drain(r2.at[pl.ds(0, 2), pl.ds(0, 6)], q1_send.at[b])
            drain(r2.at[pl.ds(0, 2), pl.ds(0, 6)], q1_send.at[b])
        else:
            drain(r2.at[pl.ds(0, n), pl.ds(0, 7)], q1_send.at[b])
            drain(q_ref.at[:, pl.ds(0, 3), :, :, q_cols(b)], q2_send.at[b])

    for g in range(STAGED):
        drain(r1.at[g, pl.ds(0, 3)], o1_send.at[g])
        drain(l1.at[g, pl.ds(0, 3)], l1_send.at[g])
        drain(r2.at[g, pl.ds(0, 7)], o2_send.at[g])
        drain(l2.at[g, pl.ds(0, 7)], l2_send.at[g])
        drain(r2.at[g, pl.ds(0, 7)], a1_send.at[g])
        drain(r1.at[g, pl.ds(0, 3)], a2_send.at[g])
    for j in range(GROUPS - STAGED):
        drain(d_recv.at[j, pl.ds(0, HOSTS - 1)], o1_send.at[STAGED + j])
        drain(dl_recv.at[j, pl.ds(0, HOSTS - 1)], l1_send.at[STAGED + j])
        drain(d_recv.at[j, pl.ds(0, HOSTS - 1)], a1_send.at[STAGED + j])
    for g in range(GROUPS):
        for kv in range(2):
            result(g, kv).wait()
    for i in range(3):
        drain(hd_recv.at[i], h_send.at[i])


def attention(qp, keys, values, lengths, w_out):
    vmem = pl.BlockSpec(memory_space=pltpu.VMEM)
    anywhere = pl.BlockSpec(memory_space=pl.ANY)
    bf, f32 = jnp.bfloat16, jnp.float32
    dma = pltpu.SemaphoreType.DMA
    nq, n = len(Q_BATCHES), GROUPS
    scratch = [
        ((2 * KEYS, HD), bf), ((2 * KEYS, HD), bf), ((2 * KEYS, HD), f32), ((2 * KEYS, HD), f32), ((HD, HD), bf),
        ((2048, 256), bf), ((2, KEYS, HD), bf), ((2, HD + 16, KEYS), bf), ((2, 4, 4, 16, 1024), bf),
        ((KEYS, ROWS), f32), ((KEYS, ROWS), f32),
        ((n, 2, 4, 4, 16, HD), bf), ((n, 4, 1, 128), f32), ((n, 4, 2, 4, 16, HD), bf), ((n, 4, 4, 1, 128), f32),
        ((n, 2, 4, 16, HD), bf), ((n, 4, 1, 128), f32), ((n, 8, 16, HD), bf), ((n, 8, 1, 128), f32),
        ((n - STAGED, HOSTS, 16, HD), bf), ((n - STAGED, HOSTS, 1, 128), f32),
        ((n, 2, 4, 4, 16, HD), bf), ((128, 128), f32), ((128, 128), f32),
        ((ROWS, 256), f32), ((ROWS, 256), bf), ((3, 64, 256), bf),
    ]
    sems = [3, n, nq, nq, nq, nq] + [n] * 12 + [3, 3]
    att, proj = pl.pallas_call(
        main_kernel,
        out_shape=(jax.ShapeDtypeStruct((4, 4, 16, 2048), bf), jax.ShapeDtypeStruct((64, 256), bf)),
        in_specs=[vmem, anywhere, anywhere, pl.BlockSpec(memory_space=pltpu.SMEM), anywhere],
        out_specs=(anywhere, vmem),
        scratch_shapes=[pltpu.VMEM(*s) for s in scratch] + [dma((k,)) for k in sems],
        compiler_params=pltpu.CompilerParams(
            collective_id=0, has_side_effects=True, vmem_limit_bytes=56 << 20
        ),
    )(qp, keys.reshape(2 * KEYS, HD), values.reshape(2 * KEYS, HD), lengths, w_out)
    return settle(att.reshape(ROWS, 2048), proj)


def settle_kernel(att_ref, proj_ref, att_out, proj_out):
    att_out[...] = att_ref[...]
    proj_out[...] = proj_ref[...]


def settle(att, proj):
    blocks = (pl.BlockSpec((128, 2048), lambda i: (i, 0)), pl.BlockSpec((32, 256), lambda i: (i, 0)))
    return pl.pallas_call(
        settle_kernel,
        grid=(2,),
        out_shape=(jax.ShapeDtypeStruct(att.shape, att.dtype), jax.ShapeDtypeStruct(proj.shape, proj.dtype)),
        in_specs=list(blocks),
        out_specs=blocks,
    )(att, proj)


def body(queries, keys, values, lengths, owner, w_out):
    qp = lax.switch(owner[0], [functools.partial(scatter, o) for o in range(HOSTS)], queries)
    return attention(qp, keys, values, lengths, w_out)


def solution(mesh):
    in_specs = (
        P("ctx", None, "head"),
        P("ctx", "head", None),
        P("ctx", "head", None),
        P("ctx"),
        P(),
        P("head", "ctx"),
    )
    out_specs = (P(None, "head"), P("head", "ctx"))
    return jax.shard_map(body, mesh=mesh, in_specs=in_specs, out_specs=out_specs, check_vma=False)
```

```python
import functools
import math

import jax
import jax.numpy as jnp
from jax import lax
from jax.experimental import pallas as pl
from jax.experimental.pallas import tpu as pltpu
from jax.sharding import PartitionSpec as P

MESH = pl.DeviceIdType.MESH
HOSTS = 32
GROUPS = 8
ROWS = 256
HD = 128
KEYS = 4096
CHUNK = 1024
SCALE = math.log2(math.e) / math.sqrt(HD)
STAGED = 4
DIRECT = ((4, 2), (6, 1), (7, 1))
AFTER = (0, 2, 4, 6, 8)
OTHERS = sorted(
    ((dy, dx, dz) for dy in range(2) for dx in range(4) for dz in range(4) if (dy, dx, dz) != (0, 0, 0)),
    key=lambda d: -(2 * d[0] + min(d[1], 4 - d[1]) + min(d[2], 4 - d[2])),
)
Q_BATCHES = ((0, 2, False), (2, 5, False), (5, 8, True))


def remote(src, dst, send, recv, ctx):
    return pltpu.make_async_remote_copy(
        src_ref=src, dst_ref=dst, send_sem=send, recv_sem=recv, device_id=ctx, device_id_type=MESH
    )


def drain(ref, sem):
    pltpu.make_async_copy(ref, ref, sem).wait()


def scatter_kernel(owner, q_ref, out_ref, send, recv):
    me = lax.axis_index("ctx")
    barrier = pltpu.get_barrier_semaphore()

    @pl.when(me != owner)
    def _():
        pl.semaphore_signal(barrier, inc=1, device_id={"ctx": owner}, device_id_type=MESH)
        drain(out_ref, recv)

    @pl.when(me == owner)
    def _():
        pl.semaphore_wait(barrier, HOSTS - 1)

        def piece(p):
            return q_ref.at[0, pl.ds(16 * (p % 16), 16), pl.ds(1024 * (p // 16), 1024)]

        copies = []
        for step, (dy, dx, dz) in enumerate(OTHERS, 1):
            p = 16 * ((owner // 16 + dy) % 2) + 4 * ((owner // 4 + dx) % 4) + (owner + dz) % 4
            copies.append(remote(piece(p), out_ref, send.at[step], recv, {"ctx": p}))
            copies[-1].start()
        own = pltpu.make_async_copy(piece(owner), out_ref, send.at[0])
        own.start()
        own.wait()
        for copy in copies:
            copy.wait_send()


def scatter(owner, queries):
    return pl.pallas_call(
        functools.partial(scatter_kernel, owner),
        out_shape=jax.ShapeDtypeStruct((16, 1024), jnp.bfloat16),
        in_specs=[pl.BlockSpec(memory_space=pl.ANY)],
        out_specs=pl.BlockSpec(memory_space=pltpu.VMEM),
        scratch_shapes=[pltpu.SemaphoreType.DMA((HOSTS,)), pltpu.SemaphoreType.DMA],
        compiler_params=pltpu.CompilerParams(collective_id=owner + 1, has_side_effects=True),
    )(queries)


def main_kernel(
    qp_ref, k_hbm, v_hbm, len_ref, w_hbm, att_hbm, proj_ref,
    k_in, v_in, k_wide, v_wide, eye, w_ref, k_ref, vt_ref, q_ref, sa, sb,
    o_buf, l_buf, r1, l1, s2, l2_buf, r2, l2, d_recv, dl_recv, at_buf, w1, w2, part, hd_buf, hd_recv,
    local_sem, out_sem, q1_send, q1_recv, q2_send, q2_recv, o1_send, o1_recv, l1_send, l1_recv,
    o2_send, o2_recv, l2_send, l2_recv, a1_send, a1_recv, a2_send, a2_recv, h_send, h_recv,
):
    me = lax.axis_index("ctx")
    hd = lax.axis_index("head")
    y, x, z = me // 16, lax.rem(me // 4, 4), lax.rem(me, 4)
    loads = [
        pltpu.make_async_copy(k_hbm, k_in, local_sem.at[0]),
        pltpu.make_async_copy(v_hbm, v_in, local_sem.at[1]),
        pltpu.make_async_copy(w_hbm, w_ref, local_sem.at[2]),
    ]
    for load in loads:
        load.start()
    barrier = pltpu.get_barrier_semaphore()
    for i in range(1, HOSTS):
        pl.semaphore_signal(barrier, inc=1, device_id={"ctx": lax.rem(me + i, HOSTS)}, device_id_type=MESH)
    for i in range(1, 4):
        pl.semaphore_signal(barrier, inc=1, device_id={"head": lax.rem(hd + i, 4)}, device_id_type=MESH)
    count = len_ref[0]
    loads[0].wait()
    for c in range(KEYS // 512):
        at = 512 * c
        k_wide[2 * at : 2 * at + 1024, :] = k_in[2 * at : 2 * at + 1024, :].astype(jnp.float32)
        row = lax.broadcasted_iota(jnp.int32, (512, HD), 0) + at
        for kv in range(2):
            k_ref[kv, at : at + 512, :] = jnp.where(
                row < count, k_wide[pl.ds(2 * at + kv, 512, stride=2), :], k_wide[kv : kv + 1, :]
            ).astype(jnp.bfloat16)
    pl.semaphore_wait(barrier, HOSTS - 1 + 3)

    def others():
        for dy, dx, dz in OTHERS:
            yield lax.rem(y + dy, 2), lax.rem(x + dx, 4), lax.rem(z + dz, 4)

    def q_cols(b):
        first, last, _ = Q_BATCHES[b]
        return pl.ds(first * HD, (last - first) * HD)

    def q_plane(b):
        cols = q_cols(b)
        return q_ref.at[:, x, :, :, cols] if Q_BATCHES[b][2] else q_ref.at[:, :, z, :, cols]

    for b in range(len(Q_BATCHES)):
        src, dst = qp_ref.at[:, q_cols(b)], q_ref.at[y, x, z, :, q_cols(b)]
        if b == 0:
            for yy, xx, zz in others():
                remote(src, dst, q1_send.at[b], q1_recv.at[b], {"ctx": 16 * yy + 4 * xx + zz}).start()
        for i in range(1, 8) if b else ():
            if Q_BATCHES[b][2]:
                q = lax.rem(4 * y + z + i, 8)
                to = 16 * (q // 4) + 4 * x + lax.rem(q, 4)
            else:
                q = lax.rem(4 * y + x + i, 8)
                to = 16 * (q // 4) + 4 * lax.rem(q, 4) + z
            remote(src, dst, q1_send.at[b], q1_recv.at[b], {"ctx": to}).start()
        pltpu.make_async_copy(src, dst, q1_recv.at[b]).start()

    def q_ring(b):
        drain(q_plane(b), q1_recv.at[b])
        for i in range(1, 4):
            to = 16 * y + 4 * lax.rem(x + i, 4) + z if Q_BATCHES[b][2] else 16 * y + 4 * x + lax.rem(z + i, 4)
            remote(q_plane(b), q_plane(b), q2_send.at[b], q2_recv.at[b], {"ctx": to}).start()

    def q_ready(b):
        drain(q_ref.at[:, pl.ds(0, 3), :, :, q_cols(b)], q2_recv.at[b])

    loads[1].wait()
    eye[...] = jnp.where(
        lax.broadcasted_iota(jnp.int32, (HD, HD), 0) == lax.broadcasted_iota(jnp.int32, (HD, HD), 1), 1.0, 0.0
    ).astype(jnp.bfloat16)
    for c in range(KEYS // 512):
        at = 512 * c
        v_wide[2 * at : 2 * at + 1024, :] = v_in[2 * at : 2 * at + 1024, :].astype(jnp.float32)
        row = lax.broadcasted_iota(jnp.int32, (512, HD), 0) + at
        col = lax.broadcasted_iota(jnp.int32, (16, 512), 1) + at
        for kv in range(2):
            v = jnp.where(row < count, v_wide[pl.ds(2 * at + kv, 512, stride=2), :], 0.0).astype(jnp.bfloat16)
            vt_ref[kv, 0:HD, at : at + 512] = lax.dot_general(
                eye[...], v, (((1,), (1,)), ((), ())), preferred_element_type=jnp.float32
            ).astype(jnp.bfloat16)
            vt_ref[kv, HD : HD + 16, at : at + 512] = jnp.where(col < count, 1.0, 0.0).astype(jnp.bfloat16)
    for b in range(1, len(Q_BATCHES)):
        q_ring(b)

    def head_q(g, kv):
        return q_ref[kv, :, :, :, pl.ds(pl.multiple_of(g * HD, HD), HD)].reshape(ROWS, HD)

    def scores(kv, c, q, s_ref, top):
        at = c * CHUNK
        s = lax.dot_general(
            k_ref[kv, at : at + CHUNK, :], q, (((1,), (1,)), ((), ())), preferred_element_type=jnp.float32
        )
        s_ref[at : at + CHUNK, :] = s
        return jnp.maximum(top, jnp.max(s.reshape(CHUNK // 8, 8, ROWS), axis=0))

    def weigh(kv, c, s_ref, top, acc):
        at = c * CHUNK
        p = jnp.exp2(s_ref[at : at + CHUNK, :] * SCALE - top).astype(jnp.bfloat16)
        return acc + jnp.dot(vt_ref[kv, 0 : HD + 8, at : at + CHUNK], p, preferred_element_type=jnp.float32)

    def finish(g, kv, acc, top):
        total = acc[HD : HD + 1]
        o_buf[g, kv] = (acc[:HD] * (1.0 / total)).astype(jnp.bfloat16).T.reshape(4, 4, 16, HD)
        lse = top + jnp.log2(total)
        l_buf[g, 2 * kv] = lse[:, :128]
        l_buf[g, 2 * kv + 1] = lse[:, 128:]

    low = jnp.full((8, ROWS), -jnp.inf, jnp.float32)
    zero = jnp.zeros((HD + 8, ROWS), jnp.float32)

    def attend(g, best):
        top = jnp.max(best, axis=0, keepdims=True) * SCALE
        q = head_q(g, 1)
        other, acc = low, zero
        for c in range(KEYS // CHUNK):
            other = scores(1, c, q, sb, other)
            acc = weigh(0, c, sa, top, acc)
        finish(g, 0, acc, top)
        top = jnp.max(other, axis=0, keepdims=True) * SCALE
        q = head_q(jnp.minimum(g + 1, GROUPS - 1), 0)
        best, acc = low, zero
        for c in range(KEYS // CHUNK):
            best = scores(0, c, q, sa, best)
            acc = weigh(1, c, sb, top, acc)
        finish(g, 1, acc, top)
        return best

    def place(g):
        odd = lax.rem(g, 2)
        a, b = x + odd * (z - x), z + odd * (x - z)

        def host(yy, aa, bb):
            return {"ctx": 16 * yy + (4 - 3 * odd) * aa + (1 + 3 * odd) * bb}

        return a, b, host

    def plane(g):
        a, b, host = place(g)
        for i in range(1, 8):
            q = lax.rem(4 * y + a + i, 8)
            yield q // 4, lax.rem(q, 4), host(q // 4, lax.rem(q, 4), b)

    def ring(g):
        a, b, host = place(g)
        for i in range(1, 4):
            bb = lax.rem(b + i, 4)
            yield bb, host(y, a, bb)

    def send_ring(g):
        a, b, _ = place(g)
        for bb, to in ring(g):
            remote(l_buf.at[g], l1.at[g, b], l1_send.at[g], l1_recv.at[g], to).start()
            remote(o_buf.at[g, :, :, bb], r1.at[g, b], o1_send.at[g], o1_recv.at[g], to).start()
        pltpu.make_async_copy(l_buf.at[g], l1.at[g, b], l1_recv.at[g]).start()
        pltpu.make_async_copy(o_buf.at[g, :, :, b], r1.at[g, b], o1_recv.at[g]).start()

    def combine_ring(g):
        a, b, _ = place(g)
        drain(l1.at[g], l1_recv.at[g])
        lse = l1[g, :, :, 0, :]
        top = jnp.max(lse, axis=0)
        w = jnp.exp2(lse - top[None])
        total = jnp.sum(w, axis=0)
        w = (w / total[None]).reshape(16, 128)
        w1[...] = jnp.concatenate([w, jnp.zeros((112, 128), jnp.float32)], 0).T
        l2_buf[g, :, 0, :] = top + jnp.log2(total)
        drain(r1.at[g], o1_recv.at[g])
        for aa in range(4):
            ws = w1[pl.ds(pl.multiple_of(64 * (aa % 2) + 16 * b, 16), 16), :]
            for yy in range(2):
                acc = jnp.zeros((16, HD), jnp.float32)
                for src in range(4):
                    at = 4 * src + 2 * yy + aa // 2
                    acc = acc + ws[:, at : at + 1] * r1[g, src, yy, aa].astype(jnp.float32)
                s2[g, yy, aa] = acc.astype(jnp.bfloat16)
        mine = 4 * y + a
        for yy, aa, to in plane(g):
            remote(l2_buf.at[g, 2 * yy + aa // 2], l2.at[g, mine], l2_send.at[g], l2_recv.at[g], to).start()
            remote(s2.at[g, yy, aa], r2.at[g, mine], o2_send.at[g], o2_recv.at[g], to).start()
        pltpu.make_async_copy(l2_buf.at[g, 2 * y + a // 2], l2.at[g, mine], l2_recv.at[g]).start()
        pltpu.make_async_copy(s2.at[g, y, a], r2.at[g, mine], o2_recv.at[g]).start()

    def combine_plane(g):
        a, b, _ = place(g)
        drain(l2.at[g], l2_recv.at[g])
        lse = l2[g, :, 0, :]
        w = jnp.exp2(lse - jnp.max(lse, axis=0, keepdims=True))
        w = w / jnp.sum(w, axis=0, keepdims=True)
        w2[...] = jnp.concatenate([w, jnp.zeros((120, 128), jnp.float32)], 0).T
        drain(r2.at[g], o2_recv.at[g])
        ws = w2[pl.ds(pl.multiple_of(64 * lax.rem(a, 2) + 16 * b, 16), 16), :]
        acc = jnp.zeros((16, HD), jnp.float32)
        for src in range(8):
            acc = acc + ws[:, src : src + 1] * r2[g, src].astype(jnp.float32)
        at_buf[g, y, a, b] = acc.astype(jnp.bfloat16)
        own = at_buf.at[g, y, a, b]
        for _, _, to in plane(g):
            remote(own, own, a1_send.at[g], a1_recv.at[g], to).start()

    def gather_ring(g):
        a, b, _ = place(g)
        drain(r2.at[g, pl.ds(0, 7)], a1_recv.at[g])
        for _, to in ring(g):
            own = at_buf.at[g, :, :, b]
            remote(own, own, a2_send.at[g], a2_recv.at[g], to).start()

    def result(g, kv):
        return pltpu.make_async_copy(
            at_buf.at[g, kv], att_hbm.at[:, :, :, pl.ds(pl.multiple_of(kv * 1024 + g * HD, HD), HD)], out_sem.at[g]
        )

    def project(g):
        drain(r1.at[g, pl.ds(0, 3)], a2_recv.at[g])
        multiply(g)

    def multiply(g):
        for kv in range(2):
            result(g, kv).start()
            rows = pl.ds(pl.multiple_of(kv * 1024 + g * HD, HD), HD)
            part[...] += jnp.dot(
                at_buf[g, kv].reshape(ROWS, HD), w_ref[rows, :], preferred_element_type=jnp.float32
            )

    stages = (send_ring, combine_ring, combine_plane, gather_ring, project)

    def send_direct(g, n):
        at, to = pl.ds(g, n), pl.ds(g - STAGED, n)
        for yy, xx, zz in others():
            p = {"ctx": 16 * yy + 4 * xx + zz}
            remote(
                l_buf.at[at, 2 * yy + xx // 2], dl_recv.at[to, me], l1_send.at[g], l1_recv.at[g], p
            ).start()
            remote(o_buf.at[at, yy, xx, zz], d_recv.at[to, me], o1_send.at[g], o1_recv.at[g], p).start()
        pltpu.make_async_copy(l_buf.at[at, me // 8], dl_recv.at[to, me], l1_recv.at[g]).start()
        pltpu.make_async_copy(o_buf.at[at, y, x, z], d_recv.at[to, me], o1_recv.at[g]).start()

    def combine_direct(g, n):
        to = pl.ds(g - STAGED, n)
        drain(dl_recv.at[to], l1_recv.at[g])
        drain(d_recv.at[to], o1_recv.at[g])
        for k in range(n):
            j = g - STAGED + k
            lse = dl_recv[j, :, 0, :]
            w = jnp.exp2(lse - jnp.max(lse, axis=0, keepdims=True))
            w = w / jnp.sum(w, axis=0, keepdims=True)
            w2[...] = jnp.concatenate([w, jnp.zeros((96, 128), jnp.float32)], 0).T
            ws = w2[pl.ds(pl.multiple_of(64 * lax.rem(x, 2) + 16 * z, 16), 16), :]
            acc = jnp.zeros((16, HD), jnp.float32)
            for src in range(HOSTS):
                acc = acc + ws[:, src : src + 1] * d_recv[j, src].astype(jnp.float32)
            at_buf[g + k, y, x, z] = acc.astype(jnp.bfloat16)
        own = at_buf.at[pl.ds(g, n), y, x, z]
        for yy, xx, zz in others():
            remote(own, own, a1_send.at[g], a1_recv.at[g], {"ctx": 16 * yy + 4 * xx + zz}).start()

    def project_direct(g, n):
        drain(d_recv.at[pl.ds(g - STAGED, n), pl.ds(0, HOSTS - 1)], a1_recv.at[g])
        for k in range(n):
            multiply(g + k)

    def exchange(g):
        for n in reversed(range(len(stages))):
            @pl.when((g >= AFTER[n]) & (g < STAGED + AFTER[n]))
            def _():
                stages[n](g - AFTER[n])

    part[...] = jnp.zeros_like(part)
    drain(q_ref.at[:, :, :, :, q_cols(0)], q1_recv.at[0])
    q = head_q(0, 0)
    best = low
    for c in range(KEYS // CHUNK):
        best = scores(0, c, q, sa, best)
    loads[2].wait()

    def step(g, best):
        for b in range(1, len(Q_BATCHES)):
            @pl.when(g == Q_BATCHES[b][0] - 1)
            def _():
                q_ready(b)

        best = attend(g, best)

        for first, n in DIRECT:
            @pl.when(g == first + n - 1)
            def _():
                send_direct(first, n)

        @pl.when(g == GROUPS - 1)
        def _():
            combine_direct(*DIRECT[0])

        exchange(g)
        return best

    lax.fori_loop(0, GROUPS, step, best)

    combine_direct(*DIRECT[1])
    for n in range(1, len(stages)):
        for g in range(STAGED):
            if GROUPS <= g + AFTER[n]:
                stages[n](g)
        if n == 1:
            combine_direct(*DIRECT[2])
    for first, n in DIRECT:
        project_direct(first, n)

    hd_buf[...] = part[...].astype(jnp.bfloat16)
    for i in (1, 2, 3):
        to = lax.rem(hd + i, 4)
        for n in range(4):
            remote(
                hd_buf.at[pl.ds(pl.multiple_of(64 * to + 16 * n, 16), 16), :], hd_recv.at[i - 1, pl.ds(16 * n, 16)],
                h_send.at[i - 1], h_recv.at[i - 1], {"head": to},
            ).start()
    total = part[pl.ds(pl.multiple_of(64 * hd, 64), 64), :]
    for i in range(3):
        drain(hd_recv.at[i], h_recv.at[i])
        total = total + hd_recv[i].astype(jnp.float32)
    proj_ref[...] = total.astype(jnp.bfloat16)

    for b in range(len(Q_BATCHES)):
        n = Q_BATCHES[b][1] - Q_BATCHES[b][0]
        if b == 0:
            drain(o_buf.at[pl.ds(0, 2), 0, pl.ds(0, 3)], q1_send.at[b])
            drain(r2.at[pl.ds(0, 2), pl.ds(0, 7)], q1_send.at[b])
            drain(r2.at[pl.ds(0, 2), pl.ds(0, 6)], q1_send.at[b])
            drain(r2.at[pl.ds(0, 2), pl.ds(0, 6)], q1_send.at[b])
        else:
            drain(r2.at[pl.ds(0, n), pl.ds(0, 7)], q1_send.at[b])
            drain(q_ref.at[:, pl.ds(0, 3), :, :, q_cols(b)], q2_send.at[b])

    for g in range(STAGED):
        drain(r1.at[g, pl.ds(0, 3)], o1_send.at[g])
        drain(l1.at[g, pl.ds(0, 3)], l1_send.at[g])
        drain(r2.at[g, pl.ds(0, 7)], o2_send.at[g])
        drain(l2.at[g, pl.ds(0, 7)], l2_send.at[g])
        drain(r2.at[g, pl.ds(0, 7)], a1_send.at[g])
        drain(r1.at[g, pl.ds(0, 3)], a2_send.at[g])
    for first, n in DIRECT:
        sent = pl.ds(first - STAGED, n), pl.ds(0, HOSTS - 1)
        drain(d_recv.at[sent], o1_send.at[first])
        drain(dl_recv.at[sent], l1_send.at[first])
        drain(d_recv.at[sent], a1_send.at[first])
    for g in range(GROUPS):
        for kv in range(2):
            result(g, kv).wait()
    for i in range(3):
        drain(hd_recv.at[i], h_send.at[i])


def attention(qp, keys, values, lengths, w_out):
    vmem = pl.BlockSpec(memory_space=pltpu.VMEM)
    anywhere = pl.BlockSpec(memory_space=pl.ANY)
    bf, f32 = jnp.bfloat16, jnp.float32
    dma = pltpu.SemaphoreType.DMA
    nq, n = len(Q_BATCHES), GROUPS
    scratch = [
        ((2 * KEYS, HD), bf), ((2 * KEYS, HD), bf), ((2 * KEYS, HD), f32), ((2 * KEYS, HD), f32), ((HD, HD), bf),
        ((2048, 256), bf), ((2, KEYS, HD), bf), ((2, HD + 16, KEYS), bf), ((2, 4, 4, 16, 1024), bf),
        ((KEYS, ROWS), f32), ((KEYS, ROWS), f32),
        ((n, 2, 4, 4, 16, HD), bf), ((n, 4, 1, 128), f32), ((n, 4, 2, 4, 16, HD), bf), ((n, 4, 4, 1, 128), f32),
        ((n, 2, 4, 16, HD), bf), ((n, 4, 1, 128), f32), ((n, 8, 16, HD), bf), ((n, 8, 1, 128), f32),
        ((n - STAGED, HOSTS, 16, HD), bf), ((n - STAGED, HOSTS, 1, 128), f32),
        ((n, 2, 4, 4, 16, HD), bf), ((128, 128), f32), ((128, 128), f32),
        ((ROWS, 256), f32), ((ROWS, 256), bf), ((3, 64, 256), bf),
    ]
    sems = [3, n, nq, nq, nq, nq] + [n] * 12 + [3, 3]
    att, proj = pl.pallas_call(
        main_kernel,
        out_shape=(jax.ShapeDtypeStruct((4, 4, 16, 2048), bf), jax.ShapeDtypeStruct((64, 256), bf)),
        in_specs=[vmem, anywhere, anywhere, pl.BlockSpec(memory_space=pltpu.SMEM), anywhere],
        out_specs=(anywhere, vmem),
        scratch_shapes=[pltpu.VMEM(*s) for s in scratch] + [dma((k,)) for k in sems],
        compiler_params=pltpu.CompilerParams(
            collective_id=0, has_side_effects=True, vmem_limit_bytes=56 << 20
        ),
    )(qp, keys.reshape(2 * KEYS, HD), values.reshape(2 * KEYS, HD), lengths, w_out)
    return settle(att.reshape(ROWS, 2048), proj)


def settle_kernel(att_ref, proj_ref, att_out, proj_out):
    att_out[...] = att_ref[...]
    proj_out[...] = proj_ref[...]


def settle(att, proj):
    blocks = (pl.BlockSpec((128, 2048), lambda i: (i, 0)), pl.BlockSpec((32, 256), lambda i: (i, 0)))
    return pl.pallas_call(
        settle_kernel,
        grid=(2,),
        out_shape=(jax.ShapeDtypeStruct(att.shape, att.dtype), jax.ShapeDtypeStruct(proj.shape, proj.dtype)),
        in_specs=list(blocks),
        out_specs=blocks,
    )(att, proj)


def body(queries, keys, values, lengths, owner, w_out):
    qp = lax.switch(owner[0], [functools.partial(scatter, o) for o in range(HOSTS)], queries)
    return attention(qp, keys, values, lengths, w_out)


def solution(mesh):
    in_specs = (
        P("ctx", None, "head"),
        P("ctx", "head", None),
        P("ctx", "head", None),
        P("ctx"),
        P(),
        P("head", "ctx"),
    )
    out_specs = (P(None, "head"), P("head", "ctx"))
    return jax.shard_map(body, mesh=mesh, in_specs=in_specs, out_specs=out_specs, check_vma=False)
```
